32 devices in a mesh: grp: 4 (over y, core), wide: 8 (over z, x).
Axes of the slice: x: 2, y: 2, z: 4, core: 2. Of those that a mesh axis runs over, the one named last changes fastest.
Arguments:
- codes: bfloat16 [768, 16384], P(('grp', 'wide')), may hold values from -6 to 6
- exponents: int32 [768], P(('grp', 'wide')), may hold values from -2 to 1
- precond: bfloat16 [16384, 16384], P(None, 'wide')
- partner: int32 [4], replicated, may hold values from 0 to 3, each once
Outputs:
- kernel_diag: float32 [768, 192], P(('grp', 'wide'))
- kernel_pair: float32 [768, 192], P(('grp', 'wide'))
- kernel_back: float32 [768, 192], P(('grp', 'wide'))
The draws below stay inside these ranges and needn't reach their ends.
Inputs may be any that keep to these rules, and one draw needn't show every extreme that they name: `partner`: every row group index appears exactly once.
All inputs are finite; a program needn't handle non-finite values.
Results may differ from the reference program's by a relative error of at most 0.0029.
Values may be sent and summed in bfloat16 or wider, within the bound.
No kernel may reach another device: no remote copies, remote signals or barrier semaphores. Data moves between devices by JAX's collectives and lax.ppermute only.
A program may use at most 128 MiB of HBM per device.

```python
import math
import jax
import jax.numpy as jnp
from jax import lax

F = 16384
N = 768
N_GRP = 4


def draw_precond(key, part):
    key_off, key_diag = jax.random.split(key)
    mixed = jax.random.normal(key_off, (F, F), jnp.float32) * (0.5 / jnp.sqrt(jnp.float32(F)))
    diag_vals = jax.random.uniform(key_diag, (F,), jnp.float32, 1.8, 3.0)
    sym = mixed + mixed.T
    row_ids = lax.broadcasted_iota(jnp.int32, (F, F), 0)
    col_ids = lax.broadcasted_iota(jnp.int32, (F, F), 1)
    full = jnp.where(row_ids == col_ids, diag_vals[:, None], sym)
    return full.astype(jnp.bfloat16)


def plant(values, own_key, smallest, high):
    place = [jax.random.randint(jax.random.fold_in(own_key, axis), (), 0, length) for axis, length in enumerate(values.shape)]
    widest = values.shape.index(max(values.shape))
    next_to = place[:widest] + [(place[widest] + 1) % values.shape[widest]] + place[widest + 1:]
    return values.at[tuple(place)].set(smallest).at[tuple(next_to)].set(high)


def block_scale(rng, extent, cuts, low, top_value):
    level = 1.0
    for axis_at, blocks in cuts:
        steps = jax.random.uniform(jax.random.fold_in(jax.random.fold_in(rng, 6), axis_at), (blocks,), jnp.float32, low / len(cuts), top_value / len(cuts))
        level = level * jnp.repeat(jnp.exp(steps), extent[axis_at] // blocks).reshape((-1,) + (1,) * (len(extent) - 1 - axis_at))
    return level


def centred(key, shape, width, bound, cuts=(), kind=jnp.bfloat16):
    entries = jax.random.normal(key, shape, jnp.float32) * width
    if len(cuts) > 0:
        entries = block_scale(key, shape, cuts, -0.22, 0.18) * entries
    return jnp.clip(entries, min=-bound, max=bound).astype(kind)


def setup_inputs(seed: int = 0) -> dict:
    seeds = jax.random.split(jax.random.key(seed), 5)
    return {
        "codes": centred(seeds[0], (N, F), 1.0, 6.0, ((0, 32),)),
        "exponents": plant(jax.random.randint(seeds[1], (N,), -2, 2), jax.random.fold_in(seeds[1], 1), -2, 1).astype(jnp.int32),
        "precond": draw_precond(jax.random.fold_in(seeds[4], 71), 0),
        "partner": jax.random.permutation(seeds[3], N_GRP).astype(jnp.int32),
    }


def reference(codes, exponents, precond, partner):
    scaled = (codes.astype(jnp.float32) * jnp.exp2(exponents.astype(jnp.float32))[:, None]).astype(jnp.bfloat16)
    proj = jnp.dot(scaled, precond, preferred_element_type=jnp.float32).astype(jnp.bfloat16)
    groups = N_GRP
    block = codes.shape[0] // groups
    factor = 1.0 / math.sqrt(F)
    proj_blocks = proj.reshape(groups, block, F)
    row_blocks = scaled.reshape(groups, block, F)

    def product(items):
        return jnp.dot(items[0], items[1].T, preferred_element_type=jnp.float32) * factor
    diag = lax.map(product, (proj_blocks, row_blocks))
    others = jnp.take(row_blocks, partner.astype(jnp.int32), axis=0)
    pair = lax.map(product, (proj_blocks, others))
    onehot = (partner[None, :] == jnp.arange(groups, dtype=jnp.int32)[:, None]).astype(jnp.float32)
    back = jnp.einsum('hg,gji->hij', onehot, pair, precision=lax.Precision.HIGHEST)
    return (diag.reshape(-1, block), pair.reshape(-1, block), back.reshape(-1, block))
```

```python
import functools
import math

import jax
import jax.numpy as jnp
from jax import lax
from jax.experimental import pallas as pl
from jax.experimental.pallas import tpu as pltpu
from jax.sharding import PartitionSpec as P

CHUNKS = 4
VMEM_LIMIT = 48 * 2**20


def snake(n):
    return list(range(0, n, 2)) + list(range(n - 1, 0, -2))


def load_rows(mat_hbm, buf, sem, chunk):
    n, depth = buf.shape[0], buf.shape[1]
    return [
        pltpu.make_async_copy(
            mat_hbm.at[pl.ds((w * CHUNKS + chunk) * depth, depth)], buf.at[w], sem.at[w]
        )
        for w in range(n)
    ]


def accumulate(chunk, rows_ref, mat_hbm, buf, sem, total_ref):
    n, depth = buf.shape[0], buf.shape[1]
    copies = load_rows(mat_hbm, buf, sem, chunk)
    for copy in copies:
        copy.start()

    def step(w, carry):
        pltpu.make_async_copy(mat_hbm.at[pl.ds(0, depth)], buf.at[w], sem.at[w]).wait()
        columns = pl.ds(pl.multiple_of(w * depth, depth), depth)
        total_ref[...] += jnp.dot(
            rows_ref[:, columns], buf[w], preferred_element_type=jnp.float32
        )
        return carry

    lax.fori_loop(0, n, step, 0)


def first_kernel(chunk, rows_ref, mat_hbm, total_ref, buf, sem):
    total_ref[...] = jnp.zeros_like(total_ref)
    accumulate(chunk, rows_ref, mat_hbm, buf, sem, total_ref)


def next_kernel(chunk, rows_ref, mat_hbm, before_ref, total_ref, buf, sem):
    total_ref[...] = before_ref[...]
    accumulate(chunk, rows_ref, mat_hbm, buf, sem, total_ref)


def contract(left, right):
    return lax.dot_general(
        left, right, (((1,), (1,)), ((), ())), preferred_element_type=jnp.float32
    )


def last_kernel(
    chunk, n, order_ref, rows_ref, mat_hbm, before_ref, own_ref, other_ref, out_ref, buf, sem, total, held, placed
):
    total[...] = before_ref[...]
    accumulate(chunk, rows_ref, mat_hbm, buf, sem, total)
    image = total[...].astype(jnp.bfloat16)
    size = image.shape[0]
    step = size // n

    def reorder(block):
        held[...] = block
        for i in range(n):
            placed[pl.ds(pl.multiple_of(order_ref[i] * step, 8), step), :] = held[i * step : (i + 1) * step, :]
        return placed[...]

    diag = reorder(reorder(contract(image, own_ref[...])).T).T
    back = reorder(reorder(contract(image, other_ref[...])).T)
    out_ref[:, :size] = diag
    out_ref[:, size : 2 * size] = back.T
    out_ref[:, 2 * size :] = back


def multiply(chunk, rows, mat, before=None, tail=None):
    size, width = rows.shape
    n = width // (mat.shape[0] // (mat.shape[0] // mat.shape[1]) // CHUNKS)
    depth = width // n
    cols = mat.shape[1]
    scratch = [pltpu.VMEM((n, depth, cols), mat.dtype), pltpu.SemaphoreType.DMA((n,))]
    whole = pl.BlockSpec(memory_space=pltpu.VMEM)
    common = dict(
        compiler_params=pltpu.CompilerParams(vmem_limit_bytes=VMEM_LIMIT),
        cost_estimate=pl.CostEstimate(
            flops=2 * size * width * cols, bytes_accessed=2 * width * cols, transcendentals=0
        ),
    )
    total = jax.ShapeDtypeStruct((size, cols), jnp.float32)
    hbm = pl.BlockSpec(memory_space=pl.ANY)
    if before is None:
        return pl.pallas_call(
            functools.partial(first_kernel, chunk),
            in_specs=[whole, hbm],
            out_specs=whole,
            out_shape=total,
            scratch_shapes=scratch,
            **common,
        )(rows, mat)
    if tail is None:
        return pl.pallas_call(
            functools.partial(next_kernel, chunk),
            in_specs=[whole, hbm, whole],
            out_specs=whole,
            out_shape=total,
            scratch_shapes=scratch,
            **common,
        )(rows, mat, before)
    order, own, other = tail
    return pl.pallas_call(
        functools.partial(last_kernel, chunk, n),
        in_specs=[pl.BlockSpec(memory_space=pltpu.SMEM), whole, hbm, whole, whole, whole],
        out_specs=whole,
        out_shape=jax.ShapeDtypeStruct((size, 3 * size), jnp.float32),
        scratch_shapes=scratch
        + [pltpu.VMEM((size, cols), jnp.float32), pltpu.VMEM((size, size), jnp.float32),
        pltpu.VMEM((size, size), jnp.float32)],
        **common,
    )(order, rows, mat, before, own, other)


def after(value, *others):
    return lax.optimization_barrier((value, *others))[0]


def fetch(value, source):
    me = lax.axis_index("grp")
    near = lax.ppermute(value, "grp", [(i, i ^ 1) for i in range(4)])
    wanted = lax.dynamic_index_in_dim(source, me ^ 2, 0, keepdims=False)
    sent = jnp.where(wanted == me, value, near)
    far = lax.ppermute(sent, "grp", [(i, i ^ 2) for i in range(4)])
    mine = lax.dynamic_index_in_dim(source, me, 0, keepdims=False)
    return jnp.where(mine == me, value, jnp.where(mine == me ^ 1, near, far))


def shards(codes, exponents, precond, partner, n):
    rows, width = codes.shape
    cols = precond.shape[1]
    depth = cols // CHUNKS
    factor = 1.0 / math.sqrt(width)
    me = lax.axis_index("wide")
    group = lax.axis_index("grp")
    ring = snake(n)
    forth = [(ring[i], ring[(i + 1) % n]) for i in range(n)]
    back = [(ring[(i + 1) % n], ring[i]) for i in range(n)]
    place = jnp.array([ring.index(i) for i in range(n)], jnp.int32)[me]

    scale = jnp.exp2(exponents.astype(jnp.float32))[:, None]
    scaled = (codes.astype(jnp.float32) * scale).astype(jnp.bfloat16)
    parts = scaled.reshape(rows, n, CHUNKS, depth)
    parts = [parts[:, :, k].reshape(rows, n * depth) for k in range(CHUNKS)]

    hops = [0]
    for s in range(1, n // 2):
        hops += [-s, s]
    hops.append(n // 2)
    order = jnp.array(ring, jnp.int32)[(place + jnp.array(hops, jnp.int32)) % n]

    gathered = [None] * CHUNKS
    half = n * depth // 2
    tie = [None, None]
    for pair in range(0, CHUNKS, 2):
        lanes = []
        for lane in range(2):
            own = parts[pair + lane]
            if tie[lane] is not None:
                own = after(own, *tie[lane])
            lanes.append((own, own, [own]))
        for _ in range(1, n // 2):
            for lane in range(2):
                up, down, held = lanes[lane]
                up, down = lax.ppermute(up, "wide", forth), lax.ppermute(down, "wide", back)
                lanes[lane] = (up, down, held + [up, down])
        for lane in range(2):
            up, down, held = lanes[lane]
            tie[lane] = (up, down)
            end = jnp.concatenate(
                [
                    lax.ppermute(up[:, :half], "wide", forth),
                    lax.ppermute(down[:, half:], "wide", back),
                ],
                axis=1,
            )
            gathered[pair + lane] = jnp.concatenate(held + [end], axis=0)

    slabs, others = [], []
    for k in range(CHUNKS):
        slabs.append(lax.dynamic_slice_in_dim(gathered[k], me * depth, depth, 1))
    for pair in range(0, CHUNKS, 2):
        others.append(fetch(jnp.concatenate(slabs[pair : pair + 2], axis=1), partner))
    own = jnp.concatenate(slabs, axis=1)
    other = jnp.concatenate(others, axis=1)

    total = None
    for k in range(CHUNKS):
        tail = (order, own, other) if k == CHUNKS - 1 else None
        total = multiply(k, gathered[k], precond, total, tail)

    sums = total.reshape(n, rows, total.shape[1])
    bit = 1
    while bit < n:
        pairs = sums.reshape(sums.shape[0] // 2, 2, rows, sums.shape[2])
        mine = (me // bit) % 2
        kept = lax.dynamic_index_in_dim(pairs, mine, 1, keepdims=False)
        given = lax.dynamic_index_in_dim(pairs, 1 - mine, 1, keepdims=False)
        sums = kept + lax.ppermute(given, "wide", [(i, i ^ bit) for i in range(n)])
        bit *= 2
    sums = sums[0] * factor
    size = n * rows
    inverse = jnp.argmax(partner == group).astype(jnp.int32)
    returned = lax.all_gather(sums[None, :, 2 * size :], "grp", axis=0, tiled=True)
    kernel_back = lax.dynamic_index_in_dim(returned, inverse, 0, keepdims=False)
    return (sums[:, :size], sums[:, size : 2 * size], kernel_back)


def solution(mesh):
    return jax.shard_map(
        functools.partial(shards, n=mesh.shape["wide"]),
        mesh=mesh,
        in_specs=(P(("grp", "wide"), None), P(("grp", "wide")), P(None, "wide"), P()),
        out_specs=(P(("grp", "wide"), None), P(("grp", "wide"), None), P(("grp", "wide"), None)),
        check_vma=False,
    )
```

```python
import functools
import math

import jax
import jax.numpy as jnp
from jax import lax
from jax.experimental import pallas as pl
from jax.experimental.pallas import tpu as pltpu
from jax.sharding import PartitionSpec as P

CHUNKS = 4
VMEM_LIMIT = 28 * 2**20
WHOLE = pl.BlockSpec(memory_space=pltpu.VMEM)
SCALARS = pl.BlockSpec(memory_space=pltpu.SMEM)
HBM = pl.BlockSpec(memory_space=pl.ANY)


def call(kernel, out_shape, in_specs, scratch=(), flops=0, moved=0):
    return pl.pallas_call(
        kernel,
        in_specs=in_specs,
        out_specs=jax.tree.map(lambda _: WHOLE, out_shape),
        out_shape=out_shape,
        scratch_shapes=list(scratch),
        compiler_params=pltpu.CompilerParams(vmem_limit_bytes=VMEM_LIMIT),
        cost_estimate=pl.CostEstimate(flops=flops, bytes_accessed=moved, transcendentals=0),
    )


def contract(left, right):
    return lax.dot_general(
        left, right, (((1,), (1,)), ((), ())), preferred_element_type=jnp.float32
    )


def stack(blocks):
    return jnp.concatenate([b.astype(jnp.float32) for b in blocks], axis=0).astype(jnp.bfloat16)


def ring_member(place, n):
    return jnp.where(place < n // 2, 2 * place, 2 * (n - 1 - place) + 1)


def snake(n):
    return list(range(0, n, 2)) + list(range(n - 1, 0, -2))


def offsets(n):
    found = [0]
    for s in range(1, n // 2):
        found += [-s, s]
    return found + [n // 2]


def cut_kernel(n, exponents_ref, codes_ref, *out_refs):
    rows, width = codes_ref.shape
    depth = width // (n * CHUNKS)
    line = lax.broadcasted_iota(jnp.int32, (rows, 128), 0)
    power = jnp.zeros((rows, 128), jnp.int32)
    for r in range(rows):
        power = jnp.where(line == r, exponents_ref[r], power)
    scale = jnp.where(power < 0, jnp.where(power < -1, 0.25, 0.5), jnp.where(power > 0, 2.0, 1.0))
    for k, out_ref in enumerate(out_refs):
        for w in range(n):
            for part in range(0, depth, 128):
                start = (w * CHUNKS + k) * depth + part
                block = codes_ref[:, start : start + 128].astype(jnp.float32) * scale
                out_ref[:, w * depth + part : w * depth + part + 128] = block.astype(jnp.bfloat16)


def cut(codes, exponents, n):
    rows, width = codes.shape
    piece = jax.ShapeDtypeStruct((rows, width // CHUNKS), jnp.bfloat16)
    return call(functools.partial(cut_kernel, n), [piece] * CHUNKS, [SCALARS, WHOLE])(
        exponents, codes
    )


def slab_kernel(depth, per, *refs):
    out_ref = refs[-1]
    me = lax.axis_index("wide")
    columns = pl.ds(pl.multiple_of(me * depth, depth), depth)
    for at, ref in enumerate(refs[:-1]):
        chunk, i = divmod(at, per)
        out_ref[i, :, chunk * depth : (chunk + 1) * depth] = ref[:, columns]


def slabs(chunks, n):
    rows, width = chunks[0][0].shape
    depth = width // n
    out = jax.ShapeDtypeStruct((n, rows, depth * len(chunks)), jnp.bfloat16)
    flat = [p for c in chunks for p in c]
    return call(functools.partial(slab_kernel, depth, n), out, [WHOLE] * len(flat))(*flat)


def accumulate(chunk, first, piece_refs, mat_hbm, buf, sem, rows, total_ref):
    count, depth, cols = buf.shape
    copies = []
    for w in range(count):
        cuts = 2 if w in (0, count - 1) and depth % 32 == 0 and depth > 256 else 1
        for part in range(cuts):
            size = depth // cuts
            start = ((first + w) * CHUNKS + chunk) * depth + part * size
            target = buf.at[w, pl.ds(part * size, size)]
            at = len(copies)
            copy = pltpu.make_async_copy(mat_hbm.at[pl.ds(start, size)], target, sem.at[at])
            copy.start()
            copies.append((w, part * size, size, copy))
    rows[...] = stack([ref[:, first * depth : (first + count) * depth] for ref in piece_refs])
    while copies:
        w, inner, size, copy = copies.pop(0)
        copy.wait()
        begin = w * depth + inner
        total_ref[...] += jnp.dot(
            rows[:, begin : begin + size], buf[w, inner : inner + size], preferred_element_type=jnp.float32
        )


def part_kernel(chunk, first, n, fresh, *refs):
    pieces, (mat_hbm, before_ref), (total_ref, buf, sem, rows) = refs[:n], refs[n : n + 2], refs[-4:]
    total_ref[...] = jnp.zeros_like(total_ref) if fresh else before_ref[...]
    accumulate(chunk, first, pieces, mat_hbm, buf, sem, rows, total_ref)


def contract_kernel(n, partner_ref, *refs):
    total_ref, own_refs, other_refs = refs[0], refs[1:3], refs[3:9]
    cross_ref, pair_ref, held, placed, chosen = refs[9:]
    image = total_ref[...].astype(jnp.bfloat16)
    size = image.shape[0]
    step = size // n
    me = lax.axis_index("wide")
    group = lax.axis_index("grp")
    place = jnp.where(me % 2 == 0, me // 2, n - 1 - me // 2)
    which = partner_ref[group]

    def reorder(block):
        held[...] = block
        for i, hop in enumerate(offsets(n)):
            to = ring_member(lax.rem(place + hop + n, n), n)
            placed[pl.ds(pl.multiple_of(to * step, 8), step), :] = held[i * step : (i + 1) * step, :]
        return placed[...]

    width = own_refs[0].shape[2]
    own = [stack([ref[i] for i in range(n)]) for ref in own_refs]
    diag = sum(contract(image[:, k * width : (k + 1) * width], own[k]) for k in range(2))
    for k in range(2):
        for flip, ref in enumerate((own_refs[k], *other_refs[3 * k : 3 * k + 3])):

            @pl.when(which == group ^ flip)
            def _():
                chosen[:, k * width : (k + 1) * width] = stack([ref[i] for i in range(n)])

    pair = contract(image, chosen[...])
    back = reorder(reorder(pair).T)
    pair_ref[...] = back
    cross_ref[:, :size] = reorder(reorder(diag).T).T
    cross_ref[:, size:] = back.T


def contractions(partner, total, own, other, n):
    size, cols = total.shape
    out = [
        jax.ShapeDtypeStruct((size, 2 * size), jnp.float32),
        jax.ShapeDtypeStruct((size, size), jnp.float32),
    ]
    square = pltpu.VMEM((size, size), jnp.float32)
    kernel = functools.partial(contract_kernel, n)
    scratch = [square, square, pltpu.VMEM((size, cols), jnp.bfloat16)]
    return call(kernel, out, [SCALARS] + [WHOLE] * 9, scratch)(partner, total, *own, *other)


def multiply(chunk, first, count, pieces, mat, before, later=()):
    n = len(pieces)
    rows, width = pieces[0].shape
    depth, size, cols = width // n, n * rows, mat.shape[1]
    total = jax.ShapeDtypeStruct((size, cols), jnp.float32)
    scratch = [
        pltpu.VMEM((count, depth, cols), mat.dtype),
        pltpu.SemaphoreType.DMA((count + 2,)),
        pltpu.VMEM((size, count * depth), jnp.bfloat16),
    ]
    flops = 2 * size * count * depth * cols * WEIGHT
    moved = 2 * count * depth * cols * WEIGHT
    fresh = before is None
    kernel = functools.partial(part_kernel, chunk, first, n, fresh)
    before = mat if fresh else before
    specs = [WHOLE] * n + [HBM, HBM if fresh else WHOLE] + [HBM] * len(later)
    return call(kernel, total, specs, scratch, flops, moved)(*pieces, mat, before, *later)


WEIGHT = 3


def after(value, *others):
    return lax.optimization_barrier((value, *others))[0]


def spread(value):
    far = lax.ppermute(value, "grp", [(i, i ^ 2) for i in range(4)])
    near = lax.ppermute(value, "grp", [(i, i ^ 1) for i in range(4)])
    return near, far


def relay(far):
    return lax.ppermute(far, "grp", [(i, i ^ 1) for i in range(4)])


def shards(codes, exponents, precond, partner, n):
    rows, width = codes.shape
    factor = 1.0 / math.sqrt(width)
    me = lax.axis_index("wide")
    group = lax.axis_index("grp")
    ring = snake(n)
    forth = [(ring[i], ring[(i + 1) % n]) for i in range(n)]
    back = [(ring[(i + 1) % n], ring[i]) for i in range(n)]

    def both_ways(lane):
        up, down, held = lane
        up, down = lax.ppermute(up, "wide", forth), lax.ppermute(down, "wide", back)
        return up, down, held + [up, down]

    def last_hops(lanes):
        one = lax.ppermute(lanes[0][0], "wide", forth)
        two = lax.ppermute(lanes[1][1], "wide", back)
        return lanes[0][2] + [one], lanes[1][2] + [two]

    parts = cut(codes, exponents, n)
    lanes = [(p, p, [p]) for p in parts[:2]]
    for _ in range(1, n // 2):
        lanes = [both_ways(lane) for lane in lanes]
    early = last_hops(lanes)
    starts = [after(p, *lane[:2]) for p, lane in zip(parts[2:], lanes)]
    lanes = [(p, p, [p]) for p in starts]

    first_own = slabs(early, n)
    first_near, first_far = spread(first_own)
    halves = [(k, h) for k in range(2) for h in range(2)]
    total = None
    steps = n // 2
    for s in range(1, steps):
        lanes = [both_ways(lane) for lane in lanes]
        while halves and len(halves) > 4 - -(-4 * s // steps):
            k, h = halves.pop(0)
            total = multiply(k, h * (n // 2), n // 2, early[k], precond, total)
        lanes = [(after(up, total), down, held) for up, down, held in lanes]
    late = last_hops(lanes)
    for k, h in halves:
        total = multiply(k, h * (n // 2), n // 2, early[k], precond, total)

    last_own = slabs([[after(p, total) for p in c] for c in late], n)
    last_near, last_far = spread(last_own)
    first_both = relay(first_far)
    total = multiply(2, 0, n, late[0], precond, total)
    total = multiply(3, 0, n // 2, late[1], precond, total)
    last_both = relay(last_far)
    total = multiply(3, n // 2, n // 2, late[1], precond, total)
    other = [first_near, first_far, first_both, last_near, last_far, last_both]
    cross, pair = contractions(partner, total, [first_own, last_own], other, n)

    sums = [block.reshape(n, rows, block.shape[1]) for block in (pair, cross)]
    bit = 1
    while bit < n:
        mine = (me // bit) % 2
        for at, block in enumerate(sums):
            pairs = block.reshape(block.shape[0] // 2, 2, *block.shape[1:])
            kept = lax.dynamic_index_in_dim(pairs, mine, 1, keepdims=False)
            given = lax.dynamic_index_in_dim(pairs, 1 - mine, 1, keepdims=False)
            sums[at] = kept + lax.ppermute(given, "wide", [(i, i ^ bit) for i in range(n)])
        bit *= 2
    size = n * rows
    cross = sums[1][0] * factor
    back_rows = sums[0][0] * factor
    kernel_back = back_rows
    for flip in (1, 2, 3):
        block = lax.ppermute(back_rows, "grp", [(i, i ^ flip) for i in range(4)])
        source = lax.dynamic_index_in_dim(partner, group ^ flip, 0, keepdims=False)
        kernel_back = jnp.where(source == group, block, kernel_back)
    return (cross[:, :size], cross[:, size:], kernel_back)


def solution(mesh):
    return jax.shard_map(
        functools.partial(shards, n=mesh.shape["wide"]),
        mesh=mesh,
        in_specs=(P(("grp", "wide"), None), P(("grp", "wide")), P(None, "wide"), P()),
        out_specs=(P(("grp", "wide"), None), P(("grp", "wide"), None), P(("grp", "wide"), None)),
        check_vma=False,
    )
```

```python
import functools
import math

import jax
import jax.numpy as jnp
from jax import lax
from jax.experimental import pallas as pl
from jax.experimental.pallas import tpu as pltpu
from jax.sharding import PartitionSpec as P

CHUNKS = 4
VMEM_LIMIT = 28 * 2**20
WHOLE = pl.BlockSpec(memory_space=pltpu.VMEM)
SCALARS = pl.BlockSpec(memory_space=pltpu.SMEM)
HBM = pl.BlockSpec(memory_space=pl.ANY)


def call(kernel, out_shape, in_specs, scratch=(), flops=0, moved=0):
    return pl.pallas_call(
        kernel,
        in_specs=in_specs,
        out_specs=jax.tree.map(lambda _: WHOLE, out_shape),
        out_shape=out_shape,
        scratch_shapes=list(scratch),
        compiler_params=pltpu.CompilerParams(vmem_limit_bytes=VMEM_LIMIT),
        cost_estimate=pl.CostEstimate(flops=flops, bytes_accessed=moved, transcendentals=0),
    )


def contract(left, right):
    return lax.dot_general(
        left, right, (((1,), (1,)), ((), ())), preferred_element_type=jnp.float32
    )


def stack(blocks):
    return jnp.concatenate([b.astype(jnp.float32) for b in blocks], axis=0).astype(jnp.bfloat16)


def ring_member(place, n):
    return jnp.where(place < n // 2, 2 * place, 2 * (n - 1 - place) + 1)


def snake(n):
    return list(range(0, n, 2)) + list(range(n - 1, 0, -2))


def offsets(n):
    found = [0]
    for s in range(1, n // 2):
        found += [-s, s]
    return found + [n // 2]


def cut_kernel(n, exponents_hbm, codes_hbm, *refs):
    out_refs, codes_ref, exponents_ref, sem = refs[:CHUNKS], *refs[CHUNKS:]
    copies = [
        pltpu.make_async_copy(codes_hbm, codes_ref, sem.at[0]),
        pltpu.make_async_copy(exponents_hbm, exponents_ref, sem.at[1]),
    ]
    for copy in copies:
        copy.start()
    for copy in copies[::-1]:
        copy.wait()
    rows, width = codes_ref.shape
    depth = width // (n * CHUNKS)
    line = lax.broadcasted_iota(jnp.int32, (rows, 128), 0)
    power = jnp.zeros((rows, 128), jnp.int32)
    for r in range(rows):
        power = jnp.where(line == r, exponents_ref[r], power)
    scale = jnp.where(power < 0, jnp.where(power < -1, 0.25, 0.5), jnp.where(power > 0, 2.0, 1.0))
    for k, out_ref in enumerate(out_refs):
        for w in range(n):
            for part in range(0, depth, 128):
                start = (w * CHUNKS + k) * depth + part
                block = codes_ref[:, start : start + 128].astype(jnp.float32) * scale
                out_ref[:, w * depth + part : w * depth + part + 128] = block.astype(jnp.bfloat16)


def cut(codes, exponents, n):
    rows, width = codes.shape
    piece = jax.ShapeDtypeStruct((rows, width // CHUNKS), jnp.bfloat16)
    scratch = [
        pltpu.VMEM(codes.shape, codes.dtype),
        pltpu.SMEM(exponents.shape, exponents.dtype),
        pltpu.SemaphoreType.DMA((2,)),
    ]
    return call(functools.partial(cut_kernel, n), [piece] * CHUNKS, [HBM, HBM], scratch)(
        exponents, codes
    )


def slab_kernel(depth, per, *refs):
    out_ref = refs[-1]
    me = lax.axis_index("wide")
    columns = pl.ds(pl.multiple_of(me * depth, depth), depth)
    for at, ref in enumerate(refs[:-1]):
        chunk, i = divmod(at, per)
        out_ref[i, :, chunk * depth : (chunk + 1) * depth] = ref[:, columns]


def slabs(chunks, n):
    rows, width = chunks[0][0].shape
    depth = width // n
    out = jax.ShapeDtypeStruct((n, rows, depth * len(chunks)), jnp.bfloat16)
    flat = [p for c in chunks for p in c]
    return call(functools.partial(slab_kernel, depth, n), out, [WHOLE] * len(flat))(*flat)


def accumulate(chunk, first, piece_refs, mat_hbm, buf, sem, rows, total_ref):
    count, depth, cols = buf.shape
    copies = []
    for w in range(count):
        cuts = 2 if w in (0, count - 1) and depth % 32 == 0 and depth > 256 else 1
        for part in range(cuts):
            size = depth // cuts
            start = ((first + w) * CHUNKS + chunk) * depth + part * size
            target = buf.at[w, pl.ds(part * size, size)]
            at = len(copies)
            copy = pltpu.make_async_copy(mat_hbm.at[pl.ds(start, size)], target, sem.at[at])
            copy.start()
            copies.append((w, part * size, size, copy))
    rows[...] = stack([ref[:, first * depth : (first + count) * depth] for ref in piece_refs])
    while copies:
        w, inner, size, copy = copies.pop(0)
        copy.wait()
        begin = w * depth + inner
        total_ref[...] += jnp.dot(
            rows[:, begin : begin + size], buf[w, inner : inner + size], preferred_element_type=jnp.float32
        )


def part_kernel(chunk, first, n, fresh, *refs):
    pieces, (mat_hbm, before_ref), (total_ref, buf, sem, rows) = refs[:n], refs[n : n + 2], refs[-4:]
    total_ref[...] = jnp.zeros_like(total_ref) if fresh else before_ref[...]
    accumulate(chunk, first, pieces, mat_hbm, buf, sem, rows, total_ref)


def contract_kernel(n, partner_ref, *refs):
    total_ref, own_refs, other_refs = refs[0], refs[1:3], refs[3:9]
    cross_ref, pair_ref, held, placed, chosen = refs[9:]
    image = total_ref[...].astype(jnp.bfloat16)
    size = image.shape[0]
    step = size // n
    me = lax.axis_index("wide")
    group = lax.axis_index("grp")
    place = jnp.where(me % 2 == 0, me // 2, n - 1 - me // 2)
    which = partner_ref[group]

    def reorder(block):
        held[...] = block
        for i, hop in enumerate(offsets(n)):
            to = ring_member(lax.rem(place + hop + n, n), n)
            placed[pl.ds(pl.multiple_of(to * step, 8), step), :] = held[i * step : (i + 1) * step, :]
        return placed[...]

    width = own_refs[0].shape[2]
    own = [stack([ref[i] for i in range(n)]) for ref in own_refs]
    diag = sum(contract(image[:, k * width : (k + 1) * width], own[k]) for k in range(2))
    for k in range(2):
        for flip, ref in enumerate((own_refs[k], *other_refs[3 * k : 3 * k + 3])):

            @pl.when(which == group ^ flip)
            def _():
                chosen[:, k * width : (k + 1) * width] = stack([ref[i] for i in range(n)])

    pair = contract(image, chosen[...])
    back = reorder(reorder(pair).T)
    pair_ref[...] = back
    cross_ref[:, :size] = reorder(reorder(diag).T).T
    cross_ref[:, size:] = back.T


def contractions(partner, total, own, other, n):
    size, cols = total.shape
    out = [
        jax.ShapeDtypeStruct((size, 2 * size), jnp.float32),
        jax.ShapeDtypeStruct((size, size), jnp.float32),
    ]
    square = pltpu.VMEM((size, size), jnp.float32)
    kernel = functools.partial(contract_kernel, n)
    scratch = [square, square, pltpu.VMEM((size, cols), jnp.bfloat16)]
    return call(kernel, out, [SCALARS] + [WHOLE] * 9, scratch)(partner, total, *own, *other)


def finish_kernel(factor, partner_ref, cross_ref, *refs):
    blocks, (diag_ref, pair_ref, back_ref) = refs[:4], refs[4:]
    group = lax.axis_index("grp")
    size = diag_ref.shape[1]
    diag_ref[...] = cross_ref[0, :, :size] * factor
    pair_ref[...] = cross_ref[0, :, size:] * factor
    for flip, block in enumerate(blocks):

        @pl.when(partner_ref[group ^ flip] == group)
        def _():
            back_ref[...] = block[0] * factor


def finish(partner, factor, cross, blocks):
    _, rows, wide = cross.shape
    out = [jax.ShapeDtypeStruct((rows, wide // 2), jnp.float32)] * 3
    kernel = functools.partial(finish_kernel, factor)
    return tuple(call(kernel, out, [SCALARS] + [WHOLE] * 5)(partner, cross, *blocks))


def multiply(chunk, first, count, pieces, mat, before, later=()):
    n = len(pieces)
    rows, width = pieces[0].shape
    depth, size, cols = width // n, n * rows, mat.shape[1]
    total = jax.ShapeDtypeStruct((size, cols), jnp.float32)
    scratch = [
        pltpu.VMEM((count, depth, cols), mat.dtype),
        pltpu.SemaphoreType.DMA((count + 2,)),
        pltpu.VMEM((size, count * depth), jnp.bfloat16),
    ]
    flops = 2 * size * count * depth * cols * WEIGHT
    moved = 2 * count * depth * cols * WEIGHT
    fresh = before is None
    kernel = functools.partial(part_kernel, chunk, first, n, fresh)
    before = mat if fresh else before
    specs = [WHOLE] * n + [HBM, HBM if fresh else WHOLE] + [HBM] * len(later)
    return call(kernel, total, specs, scratch, flops, moved)(*pieces, mat, before, *later)


WEIGHT = 3


def after(value, *others):
    return lax.optimization_barrier((value, *others))[0]


def spread(value):
    far = lax.ppermute(value, "grp", [(i, i ^ 2) for i in range(4)])
    near = lax.ppermute(value, "grp", [(i, i ^ 1) for i in range(4)])
    return near, far


def relay(far):
    return lax.ppermute(far, "grp", [(i, i ^ 1) for i in range(4)])


def shards(codes, exponents, precond, partner, n):
    rows, width = codes.shape
    factor = 1.0 / math.sqrt(width)
    me = lax.axis_index("wide")
    group = lax.axis_index("grp")
    ring = snake(n)
    forth = [(ring[i], ring[(i + 1) % n]) for i in range(n)]
    back = [(ring[(i + 1) % n], ring[i]) for i in range(n)]

    def both_ways(lane):
        up, down, held = lane
        up, down = lax.ppermute(up, "wide", forth), lax.ppermute(down, "wide", back)
        return up, down, held + [up, down]

    def last_hops(lanes):
        one = lax.ppermute(lanes[0][0], "wide", forth)
        two = lax.ppermute(lanes[1][1], "wide", back)
        return lanes[0][2] + [one], lanes[1][2] + [two]

    parts = cut(codes, exponents, n)
    lanes = [(p, p, [p]) for p in parts[:2]]
    for _ in range(1, n // 2):
        lanes = [both_ways(lane) for lane in lanes]
    early = last_hops(lanes)
    starts = [after(p, *lane[:2]) for p, lane in zip(parts[2:], lanes)]
    lanes = [(p, p, [p]) for p in starts]

    first_own = slabs(early, n)
    first_near, first_far = spread(first_own)
    halves = [(k, h) for k in range(2) for h in range(2)]
    total = None
    steps = n // 2
    for s in range(1, steps):
        lanes = [both_ways(lane) for lane in lanes]
        while halves and len(halves) > 4 - -(-4 * s // steps):
            k, h = halves.pop(0)
            total = multiply(k, h * (n // 2), n // 2, early[k], precond, total)
        lanes = [(after(lanes[0][0], total), after(lanes[0][1], total), lanes[0][2]), lanes[1]]
    late = last_hops(lanes)
    for k, h in halves:
        total = multiply(k, h * (n // 2), n // 2, early[k], precond, total)

    last_own = slabs([[after(p, total) for p in c] for c in late], n)
    last_near, last_far = spread(last_own)
    first_both = relay(first_far)
    total = multiply(2, 0, n, late[0], precond, total)
    total = multiply(3, 0, n // 2, late[1], precond, total)
    last_both = relay(last_far)
    total = multiply(3, n // 2, n // 2, late[1], precond, total)
    other = [first_near, first_far, first_both, last_near, last_far, last_both]
    cross, pair = contractions(partner, total, [first_own, last_own], other, n)

    size = n * rows
    sums = [block.reshape(n, rows, block.shape[1]) for block in (pair, cross)]
    bit = 1
    while bit < n:
        radix = 4 if 1 < bit < n // 2 else 2
        mine = (me // bit) % radix
        for at, block in enumerate(sums):
            split = block.reshape(block.shape[0] // radix, radix, *block.shape[1:])
            block = lax.dynamic_index_in_dim(split, mine, 1, keepdims=False)
            for flip in range(1, radix):
                given = lax.dynamic_index_in_dim(split, mine ^ flip, 1, keepdims=False)
                ways = [(i, i ^ flip * bit) for i in range(n)]
                if bit == 1:
                    block += lax.ppermute(given, "wide", ways)
                else:
                    block += lax.ppermute(given, "wide", ways)
            sums[at] = block
        bit *= radix
    spread_rows = [
        lax.ppermute(sums[0], "grp", [(i, i ^ flip) for i in range(4)]) for flip in (1, 2, 3)
    ]
    return finish(partner, factor, sums[1], [sums[0], *spread_rows])


def solution(mesh):
    return jax.shard_map(
        functools.partial(shards, n=mesh.shape["wide"]),
        mesh=mesh,
        in_specs=(P(("grp", "wide"), None), P(("grp", "wide")), P(None, "wide"), P()),
        out_specs=(P(("grp", "wide"), None), P(("grp", "wide"), None), P(("grp", "wide"), None)),
        check_vma=False,
    )
```

```python
import functools
import math

import jax
import jax.numpy as jnp
from jax import lax
from jax.experimental import pallas as pl
from jax.experimental.pallas import tpu as pltpu
from jax.sharding import PartitionSpec as P

CHUNKS = 4
VMEM_LIMIT = 28 * 2**20
WHOLE = pl.BlockSpec(memory_space=pltpu.VMEM)
SCALARS = pl.BlockSpec(memory_space=pltpu.SMEM)
HBM = pl.BlockSpec(memory_space=pl.ANY)


def call(kernel, out_shape, in_specs, scratch=(), flops=0, moved=0):
    return pl.pallas_call(
        kernel,
        in_specs=in_specs,
        out_specs=jax.tree.map(lambda _: WHOLE, out_shape),
        out_shape=out_shape,
        scratch_shapes=list(scratch),
        compiler_params=pltpu.CompilerParams(vmem_limit_bytes=VMEM_LIMIT),
        cost_estimate=pl.CostEstimate(flops=flops, bytes_accessed=moved, transcendentals=0),
    )


def contract(left, right):
    return lax.dot_general(
        left, right, (((1,), (1,)), ((), ())), preferred_element_type=jnp.float32
    )


def stack(blocks):
    return jnp.concatenate([b.astype(jnp.float32) for b in blocks], axis=0).astype(jnp.bfloat16)


def ring_member(place, n):
    return jnp.where(place < n // 2, 2 * place, 2 * (n - 1 - place) + 1)


def snake(n):
    return list(range(0, n, 2)) + list(range(n - 1, 0, -2))


def offsets(n):
    found = [0]
    for s in range(1, n // 2):
        found += [-s, s]
    return found + [n // 2]


def cut_kernel(n, exponents_hbm, codes_hbm, *refs):
    out_refs, codes_ref, exponents_ref, sem = refs[:CHUNKS], *refs[CHUNKS:]
    copies = [
        pltpu.make_async_copy(codes_hbm, codes_ref, sem.at[0]),
        pltpu.make_async_copy(exponents_hbm, exponents_ref, sem.at[1]),
    ]
    for copy in copies:
        copy.start()
    for copy in copies[::-1]:
        copy.wait()
    rows, width = codes_ref.shape
    depth = width // (n * CHUNKS)
    line = lax.broadcasted_iota(jnp.int32, (rows, 128), 0)
    power = jnp.zeros((rows, 128), jnp.int32)
    for r in range(rows):
        power = jnp.where(line == r, exponents_ref[r], power)
    scale = jnp.where(power < 0, jnp.where(power < -1, 0.25, 0.5), jnp.where(power > 0, 2.0, 1.0))
    for k, out_ref in enumerate(out_refs):
        for w in range(n):
            for part in range(0, depth, 128):
                start = (w * CHUNKS + k) * depth + part
                block = codes_ref[:, start : start + 128].astype(jnp.float32) * scale
                out_ref[:, w * depth + part : w * depth + part + 128] = block.astype(jnp.bfloat16)


def cut(codes, exponents, n):
    rows, width = codes.shape
    piece = jax.ShapeDtypeStruct((rows, width // CHUNKS), jnp.bfloat16)
    scratch = [
        pltpu.VMEM(codes.shape, codes.dtype),
        pltpu.SMEM(exponents.shape, exponents.dtype),
        pltpu.SemaphoreType.DMA((2,)),
    ]
    return call(functools.partial(cut_kernel, n), [piece] * CHUNKS, [HBM, HBM], scratch)(
        exponents, codes
    )


def slab_kernel(depth, per, *refs):
    out_ref = refs[-1]
    me = lax.axis_index("wide")
    columns = pl.ds(pl.multiple_of(me * depth, depth), depth)
    for at, ref in enumerate(refs[:-1]):
        chunk, i = divmod(at, per)
        out_ref[i, :, chunk * depth : (chunk + 1) * depth] = ref[:, columns]


def slabs(chunks, n):
    rows, width = chunks[0][0].shape
    depth = width // n
    out = jax.ShapeDtypeStruct((n, rows, depth * len(chunks)), jnp.bfloat16)
    flat = [p for c in chunks for p in c]
    return call(functools.partial(slab_kernel, depth, n), out, [WHOLE] * len(flat))(*flat)


def accumulate(chunk, first, piece_refs, mat_hbm, buf, sem, rows, total_ref):
    count, depth, cols = buf.shape
    copies = []
    for w in range(count):
        cuts = 2 if w in (0, count - 1) and depth % 32 == 0 and depth > 256 else 1
        for part in range(cuts):
            size = depth // cuts
            start = ((first + w) * CHUNKS + chunk) * depth + part * size
            target = buf.at[w, pl.ds(part * size, size)]
            at = len(copies)
            copy = pltpu.make_async_copy(mat_hbm.at[pl.ds(start, size)], target, sem.at[at])
            copy.start()
            copies.append((w, part * size, size, copy))
    rows[...] = stack([ref[:, first * depth : (first + count) * depth] for ref in piece_refs])
    while copies:
        w, inner, size, copy = copies.pop(0)
        copy.wait()
        begin = w * depth + inner
        total_ref[...] += jnp.dot(
            rows[:, begin : begin + size], buf[w, inner : inner + size], preferred_element_type=jnp.float32
        )


def part_kernel(chunk, first, n, fresh, *refs):
    pieces, (mat_hbm, before_ref), (total_ref, buf, sem, rows) = refs[:n], refs[n : n + 2], refs[-4:]
    total_ref[...] = jnp.zeros_like(total_ref) if fresh else before_ref[...]
    accumulate(chunk, first, pieces, mat_hbm, buf, sem, rows, total_ref)


def contract_kernel(n, partner_ref, *refs):
    total_ref, own_refs, other_refs = refs[0], refs[1:3], refs[3:9]
    cross_ref, pair_ref, held, placed, chosen = refs[9:]
    image = total_ref[...].astype(jnp.bfloat16)
    size = image.shape[0]
    step = size // n
    me = lax.axis_index("wide")
    group = lax.axis_index("grp")
    place = jnp.where(me % 2 == 0, me // 2, n - 1 - me // 2)
    which = partner_ref[group]

    def reorder(block):
        held[...] = block
        for i, hop in enumerate(offsets(n)):
            to = ring_member(lax.rem(place + hop + n, n), n)
            placed[pl.ds(pl.multiple_of(to * step, 8), step), :] = held[i * step : (i + 1) * step, :]
        return placed[...]

    width = own_refs[0].shape[2]
    own = [stack([ref[i] for i in range(n)]) for ref in own_refs]
    diag = contract(image, jnp.concatenate(own, axis=1))
    for k in range(2):
        for flip, ref in enumerate((own_refs[k], *other_refs[3 * k : 3 * k + 3])):

            @pl.when(which == group ^ flip)
            def _():
                chosen[:, k * width : (k + 1) * width] = stack([ref[i] for i in range(n)])

    pair = contract(image, chosen[...])
    back = reorder(reorder(pair).T)
    pair_ref[...] = back
    cross_ref[:, :size] = reorder(reorder(diag).T).T
    cross_ref[:, size:] = back.T


def contractions(partner, total, own, other, n):
    size, cols = total.shape
    out = [
        jax.ShapeDtypeStruct((size, 2 * size), jnp.float32),
        jax.ShapeDtypeStruct((size, size), jnp.float32),
    ]
    square = pltpu.VMEM((size, size), jnp.float32)
    kernel = functools.partial(contract_kernel, n)
    scratch = [square, square, pltpu.VMEM((size, cols), jnp.bfloat16)]
    return call(kernel, out, [SCALARS] + [WHOLE] * 9, scratch)(partner, total, *own, *other)


def finish_kernel(factor, partner_ref, cross_ref, *refs):
    blocks, (diag_ref, pair_ref, back_ref) = refs[:4], refs[4:]
    group = lax.axis_index("grp")
    size = diag_ref.shape[1]
    diag_ref[...] = cross_ref[0, :, :size] * factor
    pair_ref[...] = cross_ref[0, :, size:] * factor
    for flip, block in enumerate(blocks):

        @pl.when(partner_ref[group ^ flip] == group)
        def _():
            back_ref[...] = block[0] * factor


def finish(partner, factor, cross, blocks):
    _, rows, wide = cross.shape
    out = [jax.ShapeDtypeStruct((rows, wide // 2), jnp.float32)] * 3
    kernel = functools.partial(finish_kernel, factor)
    return tuple(call(kernel, out, [SCALARS] + [WHOLE] * 5)(partner, cross, *blocks))


def multiply(chunk, first, count, pieces, mat, before):
    n = len(pieces)
    rows, width = pieces[0].shape
    depth, size, cols = width // n, n * rows, mat.shape[1]
    total = jax.ShapeDtypeStruct((size, cols), jnp.float32)
    scratch = [
        pltpu.VMEM((count, depth, cols), mat.dtype),
        pltpu.SemaphoreType.DMA((count + 2,)),
        pltpu.VMEM((size, count * depth), jnp.bfloat16),
    ]
    flops = 2 * size * count * depth * cols * WEIGHT
    moved = 2 * count * depth * cols * WEIGHT
    fresh = before is None
    kernel = functools.partial(part_kernel, chunk, first, n, fresh)
    before = mat if fresh else before
    specs = [WHOLE] * n + [HBM, HBM if fresh else WHOLE]
    return call(kernel, total, specs, scratch, flops, moved)(*pieces, mat, before)


WEIGHT = 3


def after(value, *others):
    return lax.optimization_barrier((value, *others))[0]


def spread(value):
    far = lax.ppermute(value, "grp", [(i, i ^ 2) for i in range(4)])
    near = lax.ppermute(value, "grp", [(i, i ^ 1) for i in range(4)])
    return near, far


def relay(far):
    return lax.ppermute(far, "grp", [(i, i ^ 1) for i in range(4)])


def shards(codes, exponents, precond, partner, n):
    rows, width = codes.shape
    factor = 1.0 / math.sqrt(width)
    me = lax.axis_index("wide")
    group = lax.axis_index("grp")
    ring = snake(n)
    forth = [(ring[i], ring[(i + 1) % n]) for i in range(n)]
    back = [(ring[(i + 1) % n], ring[i]) for i in range(n)]

    def both_ways(lane):
        up, down, held = lane
        up, down = lax.ppermute(up, "wide", forth), lax.ppermute(down, "wide", back)
        return up, down, held + [up, down]

    def last_hops(lanes):
        one = lax.ppermute(lanes[0][0], "wide", forth)
        two = lax.ppermute(lanes[1][1], "wide", back)
        return lanes[0][2] + [one], lanes[1][2] + [two]

    parts = cut(codes, exponents, n)
    lanes = [(p, p, [p]) for p in parts[:2]]
    for _ in range(1, n // 2):
        before, lanes = lanes, [both_ways(lane) for lane in lanes]
    early = last_hops(lanes)
    starts = [after(parts[2], *before[1][:2]), after(parts[3], *lanes[0][:2])]
    lanes = [(p, p, [p]) for p in starts]

    first_own = slabs(early, n)
    first_near, first_far = spread(first_own)
    halves = [(k, h) for k in range(2) for h in range(2)]
    total = None
    steps = n // 2
    for s in range(1, steps):
        lanes = [both_ways(lane) for lane in lanes]
        while halves and len(halves) > 4 - -(-4 * s // steps):
            k, h = halves.pop(0)
            total = multiply(k, h * (n // 2), n // 2, early[k], precond, total)
        lanes = [(after(lanes[0][0], total), after(lanes[0][1], total), lanes[0][2]), lanes[1]]
    late = last_hops(lanes)
    for k, h in halves:
        total = multiply(k, h * (n // 2), n // 2, early[k], precond, total)

    last_own = slabs([[after(p, total) for p in c] for c in late], n)
    last_near, last_far = spread(last_own)
    first_both = relay(first_far)
    total = multiply(2, 0, n, late[0], precond, total)
    total = multiply(3, 0, n // 2, late[1], precond, total)
    last_both = relay(last_far)
    total = multiply(3, n // 2, n // 2, late[1], precond, total)
    other = [first_near, first_far, first_both, last_near, last_far, last_both]
    cross, pair = contractions(partner, total, [first_own, last_own], other, n)

    size = n * rows
    sums = [block.reshape(n, rows, block.shape[1]) for block in (pair, cross)]
    bit = 1
    while bit < n:
        radix = 4 if bit < n // 2 else 2
        mine = (me // bit) % radix
        for at, block in enumerate(sums):
            split = block.reshape(block.shape[0] // radix, radix, *block.shape[1:])
            block = lax.dynamic_index_in_dim(split, mine, 1, keepdims=False)
            for flip in range(1, radix):
                given = lax.dynamic_index_in_dim(split, mine ^ flip, 1, keepdims=False)
                ways = [(i, i ^ flip * bit) for i in range(n)]
                if bit == 1:
                    block += lax.ppermute(given, "wide", ways)
                else:
                    block += lax.ppermute(given, "wide", ways)
            sums[at] = block
        bit *= radix
    spread_rows = [
        lax.ppermute(sums[0], "grp", [(i, i ^ flip) for i in range(4)]) for flip in (1, 2, 3)
    ]
    return finish(partner, factor, sums[1], [sums[0], *spread_rows])


def solution(mesh):
    return jax.shard_map(
        functools.partial(shards, n=mesh.shape["wide"]),
        mesh=mesh,
        in_specs=(P(("grp", "wide"), None), P(("grp", "wide")), P(None, "wide"), P()),
        out_specs=(P(("grp", "wide"), None), P(("grp", "wide"), None), P(("grp", "wide"), None)),
        check_vma=False,
    )
```

```python
import functools
import math

import jax
import jax.numpy as jnp
from jax import lax
from jax.experimental import pallas as pl
from jax.experimental.pallas import tpu as pltpu
from jax.sharding import PartitionSpec as P

CHUNKS = 4
VMEM_LIMIT = 28 * 2**20
WHOLE = pl.BlockSpec(memory_space=pltpu.VMEM)
SCALARS = pl.BlockSpec(memory_space=pltpu.SMEM)
HBM = pl.BlockSpec(memory_space=pl.ANY)


def call(kernel, out_shape, in_specs, scratch=(), flops=0, moved=0):
    return pl.pallas_call(
        kernel,
        in_specs=in_specs,
        out_specs=jax.tree.map(lambda _: WHOLE, out_shape),
        out_shape=out_shape,
        scratch_shapes=list(scratch),
        compiler_params=pltpu.CompilerParams(vmem_limit_bytes=VMEM_LIMIT),
        cost_estimate=pl.CostEstimate(flops=flops, bytes_accessed=moved, transcendentals=0),
    )


def contract(left, right):
    return lax.dot_general(
        left, right, (((1,), (1,)), ((), ())), preferred_element_type=jnp.float32
    )


def stack(blocks):
    return jnp.concatenate([b.astype(jnp.float32) for b in blocks], axis=0).astype(jnp.bfloat16)


def ring_member(place, n):
    return jnp.where(place < n // 2, 2 * place, 2 * (n - 1 - place) + 1)


def snake(n):
    return list(range(0, n, 2)) + list(range(n - 1, 0, -2))


def offsets(n):
    found = [0]
    for s in range(1, n // 2):
        found += [-s, s]
    return found + [n // 2]


def cut_kernel(n, exponents_hbm, codes_hbm, *refs):
    out_refs, codes_ref, exponents_ref, sem = refs[:CHUNKS], *refs[CHUNKS:]
    copies = [
        pltpu.make_async_copy(codes_hbm, codes_ref, sem.at[0]),
        pltpu.make_async_copy(exponents_hbm, exponents_ref, sem.at[1]),
    ]
    for copy in copies:
        copy.start()
    for copy in copies[::-1]:
        copy.wait()
    rows, width = codes_ref.shape
    depth = width // (n * CHUNKS)
    line = lax.broadcasted_iota(jnp.int32, (rows, 128), 0)
    power = jnp.zeros((rows, 128), jnp.int32)
    for r in range(rows):
        power = jnp.where(line == r, exponents_ref[r], power)
    scale = jnp.where(power < 0, jnp.where(power < -1, 0.25, 0.5), jnp.where(power > 0, 2.0, 1.0))
    for k, out_ref in enumerate(out_refs):
        for w in range(n):
            for part in range(0, depth, 128):
                start = (w * CHUNKS + k) * depth + part
                block = codes_ref[:, start : start + 128].astype(jnp.float32) * scale
                out_ref[:, w * depth + part : w * depth + part + 128] = block.astype(jnp.bfloat16)


def cut(codes, exponents, n):
    rows, width = codes.shape
    piece = jax.ShapeDtypeStruct((rows, width // CHUNKS), jnp.bfloat16)
    scratch = [
        pltpu.VMEM(codes.shape, codes.dtype),
        pltpu.SMEM(exponents.shape, exponents.dtype),
        pltpu.SemaphoreType.DMA((2,)),
    ]
    return call(functools.partial(cut_kernel, n), [piece] * CHUNKS, [HBM, HBM], scratch)(
        exponents, codes
    )


def slab_kernel(depth, per, *refs):
    out_ref = refs[-1]
    me = lax.axis_index("wide")
    columns = pl.ds(pl.multiple_of(me * depth, depth), depth)
    for at, ref in enumerate(refs[:-1]):
        chunk, i = divmod(at, per)
        out_ref[i, :, chunk * depth : (chunk + 1) * depth] = ref[:, columns]


def slabs(chunks, n):
    rows, width = chunks[0][0].shape
    depth = width // n
    out = jax.ShapeDtypeStruct((n, rows, depth * len(chunks)), jnp.bfloat16)
    flat = [p for c in chunks for p in c]
    return call(functools.partial(slab_kernel, depth, n), out, [WHOLE] * len(flat))(*flat)


def accumulate(chunk, first, piece_refs, mat_hbm, buf, sem, rows, total_ref):
    count, depth, cols = buf.shape
    copies = []
    for w in range(count):
        cuts = 2 if w in (0, count - 1) and depth % 32 == 0 and depth > 256 else 1
        for part in range(cuts):
            size = depth // cuts
            start = ((first + w) * CHUNKS + chunk) * depth + part * size
            target = buf.at[w, pl.ds(part * size, size)]
            at = len(copies)
            copy = pltpu.make_async_copy(mat_hbm.at[pl.ds(start, size)], target, sem.at[at])
            copy.start()
            copies.append((w, part * size, size, copy))
    rows[...] = stack([ref[:, first * depth : (first + count) * depth] for ref in piece_refs])
    while copies:
        w, inner, size, copy = copies.pop(0)
        copy.wait()
        begin = w * depth + inner
        total_ref[...] += jnp.dot(
            rows[:, begin : begin + size], buf[w, inner : inner + size], preferred_element_type=jnp.float32
        )


def part_kernel(chunk, first, n, fresh, *refs):
    pieces, (mat_hbm, before_ref), (total_ref, buf, sem, rows) = refs[:n], refs[n : n + 2], refs[-4:]
    total_ref[...] = jnp.zeros_like(total_ref) if fresh else before_ref[...]
    accumulate(chunk, first, pieces, mat_hbm, buf, sem, rows, total_ref)


def contract_kernel(n, partner_ref, *refs):
    total_ref, own_refs, other_refs = refs[0], refs[1:3], refs[3:9]
    cross_ref, pair_ref, held, placed, chosen = refs[9:]
    image = total_ref[...].astype(jnp.bfloat16)
    size = image.shape[0]
    step = size // n
    me = lax.axis_index("wide")
    group = lax.axis_index("grp")
    place = jnp.where(me % 2 == 0, me // 2, n - 1 - me // 2)
    which = partner_ref[group]

    def reorder(block):
        held[...] = block
        for i, hop in enumerate(offsets(n)):
            to = ring_member(lax.rem(place + hop + n, n), n)
            placed[pl.ds(pl.multiple_of(to * step, 8), step), :] = held[i * step : (i + 1) * step, :]
        return placed[...]

    width = own_refs[0].shape[2]
    own = [stack([ref[i] for i in range(n)]) for ref in own_refs]
    diag = contract(image, jnp.concatenate(own, axis=1))
    for k in range(2):
        for flip, ref in enumerate((own_refs[k], *other_refs[3 * k : 3 * k + 3])):

            @pl.when(which == group ^ flip)
            def _():
                chosen[:, k * width : (k + 1) * width] = stack([ref[i] for i in range(n)])

    pair = contract(image, chosen[...])
    back = reorder(reorder(pair).T)
    pair_ref[...] = back
    cross_ref[:, :size] = reorder(reorder(diag).T).T
    cross_ref[:, size:] = back.T


def contractions(partner, total, own, other, n):
    size, cols = total.shape
    out = [
        jax.ShapeDtypeStruct((size, 2 * size), jnp.float32),
        jax.ShapeDtypeStruct((size, size), jnp.float32),
    ]
    square = pltpu.VMEM((size, size), jnp.float32)
    kernel = functools.partial(contract_kernel, n)
    scratch = [square, square, pltpu.VMEM((size, cols), jnp.bfloat16)]
    return call(kernel, out, [SCALARS] + [WHOLE] * 9, scratch)(partner, total, *own, *other)


def finish_kernel(factor, partner_ref, cross_ref, *refs):
    blocks, (diag_ref, pair_ref, back_ref) = refs[:4], refs[4:]
    group = lax.axis_index("grp")
    size = diag_ref.shape[1]
    diag_ref[...] = cross_ref[0, :, :size] * factor
    pair_ref[...] = cross_ref[0, :, size:] * factor
    for flip, block in enumerate(blocks):

        @pl.when(partner_ref[group ^ flip] == group)
        def _():
            back_ref[...] = block[0] * factor


def finish(partner, factor, cross, blocks):
    _, rows, wide = cross.shape
    out = [jax.ShapeDtypeStruct((rows, wide // 2), jnp.float32)] * 3
    kernel = functools.partial(finish_kernel, factor)
    return tuple(call(kernel, out, [SCALARS] + [WHOLE] * 5)(partner, cross, *blocks))


def multiply(chunk, first, count, pieces, mat, before):
    n = len(pieces)
    rows, width = pieces[0].shape
    depth, size, cols = width // n, n * rows, mat.shape[1]
    total = jax.ShapeDtypeStruct((size, cols), jnp.float32)
    scratch = [
        pltpu.VMEM((count, depth, cols), mat.dtype),
        pltpu.SemaphoreType.DMA((count + 2,)),
        pltpu.VMEM((size, count * depth), jnp.bfloat16),
    ]
    flops = 2 * size * count * depth * cols * WEIGHT
    moved = 2 * count * depth * cols * WEIGHT
    fresh = before is None
    kernel = functools.partial(part_kernel, chunk, first, n, fresh)
    before = mat if fresh else before
    specs = [WHOLE] * n + [HBM, HBM if fresh else WHOLE]
    return call(kernel, total, specs, scratch, flops, moved)(*pieces, mat, before)


WEIGHT = 3


def after(value, *others):
    return lax.optimization_barrier((value, *others))[0]


def spread(value):
    far = lax.ppermute(value, "grp", [(i, i ^ 2) for i in range(4)])
    near = lax.ppermute(value, "grp", [(i, i ^ 1) for i in range(4)])
    return near, far


def relay(far):
    return lax.ppermute(far, "grp", [(i, i ^ 1) for i in range(4)])


def shards(codes, exponents, precond, partner, n):
    rows, width = codes.shape
    factor = 1.0 / math.sqrt(width)
    me = lax.axis_index("wide")
    group = lax.axis_index("grp")
    ring = snake(n)
    forth = [(ring[i], ring[(i + 1) % n]) for i in range(n)]
    back = [(ring[(i + 1) % n], ring[i]) for i in range(n)]

    def both_ways(lane):
        up, down, held = lane
        up, down = lax.ppermute(up, "wide", forth), lax.ppermute(down, "wide", back)
        return up, down, held + [up, down]

    def last_hops(lanes):
        one = lax.ppermute(lanes[0][0], "wide", forth)
        two = lax.ppermute(lanes[1][1], "wide", back)
        return lanes[0][2] + [one], lanes[1][2] + [two]

    parts = cut(codes, exponents, n)
    lanes = [(p, p, [p]) for p in parts[:2]]
    for _ in range(1, n // 2):
        before, lanes = lanes, [both_ways(lane) for lane in lanes]
    early = last_hops(lanes)
    starts = [after(parts[2], *before[1][:2]), after(parts[3], *lanes[0][:2])]
    lanes = [(p, p, [p]) for p in starts]

    first_own = slabs(early, n)
    first_near, first_far = spread(first_own)
    halves = [(k, h) for k in range(2) for h in range(2)]
    total = None
    steps = n // 2
    for s in range(1, steps):
        lanes = [both_ways(lane) for lane in lanes]
        while halves and len(halves) > 4 - -(-4 * s // steps):
            k, h = halves.pop(0)
            total = multiply(k, h * (n // 2), n // 2, early[k], precond, total)
        lanes = [(after(lanes[0][0], total), after(lanes[0][1], total), lanes[0][2]), lanes[1]]
    late = last_hops(lanes)
    for k, h in halves:
        total = multiply(k, h * (n // 2), n // 2, early[k], precond, total)

    last_own = slabs([[after(p, total) for p in c] for c in late], n)
    last_near, last_far = spread(last_own)
    first_both = relay(first_far)
    total = multiply(2, 0, n, late[0], precond, total)
    total = multiply(3, 0, n // 2, late[1], precond, total)
    last_both = relay(last_far)
    total = multiply(3, n // 2, n // 2, late[1], precond, total)
    other = [first_near, first_far, first_both, last_near, last_far, last_both]
    cross, pair = contractions(partner, total, [first_own, last_own], other, n)

    size = n * rows
    sums = [jnp.concatenate([pair, cross], axis=1).reshape(n, rows, 3 * size)]
    bit = 1
    while bit < n:
        radix = 4 if bit < n // 2 else 2
        mine = (me // bit) % radix
        for at, block in enumerate(sums):
            split = block.reshape(block.shape[0] // radix, radix, *block.shape[1:])
            block = lax.dynamic_index_in_dim(split, mine, 1, keepdims=False)
            for flip in range(1, radix):
                given = lax.dynamic_index_in_dim(split, mine ^ flip, 1, keepdims=False)
                ways = [(i, i ^ flip * bit) for i in range(n)]
                if bit == 1:
                    block += lax.ppermute(given.astype(jnp.bfloat16), "wide", ways).astype(jnp.float32)
                else:
                    block += lax.ppermute(given, "wide", ways)
            sums[at] = block
        bit *= radix
        if len(sums) == 1 and (1 or bit >= n):
            sums = [sums[0][..., :size], sums[0][..., size:]]
    spread_rows = [
        lax.ppermute(sums[0], "grp", [(i, i ^ flip) for i in range(4)]) for flip in (1, 2, 3)
    ]
    return finish(partner, factor, sums[1], [sums[0], *spread_rows])


def solution(mesh):
    return jax.shard_map(
        functools.partial(shards, n=mesh.shape["wide"]),
        mesh=mesh,
        in_specs=(P(("grp", "wide"), None), P(("grp", "wide")), P(None, "wide"), P()),
        out_specs=(P(("grp", "wide"), None), P(("grp", "wide"), None), P(("grp", "wide"), None)),
        check_vma=False,
    )
```
